32 devices in a mesh: cfg: 2 (over y), slab: 4 (over z), tile: 2 (over x), spin: 2 (over core).
Axes of the slice: x: 2, y: 2, z: 4, core: 2. Of those that a mesh axis runs over, the one named last changes fastest.
Arguments:
- eigenvectors: bfloat16 [4, 2, 3, 8, 1024, 256], P(('cfg', 'tile'), None, None, 'slab', 'spin'), parts along dimension 0, may hold values from -6 to 6
- gauge_links: float32 [4, 2, 3, 3, 8, 1024], P(('cfg', 'tile'), None, None, None, 'slab', 'spin'), parts along dimension 0, may hold values from -2.5 to 2.5
- momenta: int32 [2, 3], replicated, may hold values from -2 to 2
- displacement: int32 [2], replicated, may hold values from 1 to 2, as said below
- slice_pairs: int32 [4, 2], P('tile'), may hold values from 0 to 1, as said below
- perambulators: bfloat16 [8, 2, 1024, 1024], P(('cfg', 'tile'), None, 'spin', 'slab'), parts along dimension 0, may hold values from -6 to 6
Outputs:
- meson_blocks: bfloat16 [8, 2, 1024, 1024], P(('cfg', 'tile'), None, 'spin', 'slab'), parts along dimension 0
The draws below stay inside these ranges and needn't reach their ends.
There are 2 independent parts, one for each index of `cfg`. The reference program is written for one: setup_inputs(seed, part) draws one part's arguments, and reference() takes and returns one part's arrays. A program takes and returns all parts, laid end to end along the dimension named above; an argument that names none is the same for every part. Nothing has to cross between parts.
Inputs may be any that keep to these rules, and one draw needn't show every extreme that they name: `displacement`: the entries are 1 and 2 in some order, so one elemental is displaced forward and the other backward. `slice_pairs`: column 0 is the sink slice and column 1 the source slice; every pair of slices in 0 to 1 appears exactly once.
All inputs are finite; a program needn't handle non-finite values.
Results may differ from the reference program's by a relative error of at most 0.008.
Values may be sent and summed in bfloat16 or wider, within the bound.
A program may use at most 64 MiB of HBM per device.

```python
import math
import jax
import jax.numpy as jnp
from jax import lax

NV = 256
NS = 4
ELEMS = 2
LY = 32
LZ = 32
LX = 8
NT = 2
PAIRS = 4


def draw_displacement(key, part):
    shuffled = jax.random.permutation(jax.random.fold_in(key, 7), ELEMS)
    return (1 + shuffled % 2).astype(jnp.int32)


def draw_slice_pairs(key, part):
    shuffled = jax.random.permutation(jax.random.fold_in(key, 5), PAIRS)
    return jnp.stack([shuffled // NT, shuffled % NT], axis=1).astype(jnp.int32)


def set_ends(array, stream_key, low, high):
    longest = array.shape.index(max(array.shape))
    spots = []
    for shift in (0, 1):
        where = [jax.random.randint(jax.random.fold_in(stream_key, axis), (), 0, length) for axis, length in enumerate(array.shape)]
        where[longest] = (where[longest] + shift) % array.shape[longest]
        spots.append(tuple(where))
    return array.at[spots[0]].set(low).at[spots[1]].set(high)


def levels(stream_key, shape, pieces, least, top_value):
    def one(dim, parts):
        draws = jax.random.uniform(jax.random.fold_in(jax.random.fold_in(stream_key, 6), dim), (parts,), jnp.float32, least / len(pieces), top_value / len(pieces))
        return jnp.repeat(jnp.exp(draws), shape[dim] // parts).reshape((-1,) + (1,) * (len(shape) - dim - 1))

    factor_of = one(*pieces[0])
    for cut in pieces[1:]:
        factor_of = factor_of * one(*cut)
    return factor_of


def bell_draw(own_key, extent, width, reach, shards=(), kind=jnp.bfloat16):
    gain = levels(own_key, extent, shards, -0.22, 0.18) if shards else 1.0
    values = jax.random.normal(own_key, extent, jnp.float32) * width * gain
    return jnp.minimum(jnp.maximum(values, -reach), reach).astype(kind)


def setup_inputs(seed: int = 0, part: int = 0) -> dict:
    seeds = jax.random.split(jax.random.key(seed), 7)
    part_keys = jax.random.split(jax.random.fold_in(seeds[6], part), 7)
    return {
        "eigenvectors": bell_draw(part_keys[0], (NT, 2, 3, LX, LY * LZ, NV), 1.0, 6.0, ((0, 2), (3, 4), (4, 2))),
        "gauge_links": bell_draw(part_keys[1], (NT, 2, 3, 3, LX, LY * LZ), 0.408, 2.5, ((0, 2), (4, 4), (5, 2)), jnp.float32),
        "momenta": set_ends(jax.random.randint(seeds[2], (ELEMS, 3), -2, 3), jax.random.fold_in(seeds[2], 1), -2, 2).astype(jnp.int32),
        "displacement": draw_displacement(jax.random.fold_in(seeds[6], 71), part),
        "slice_pairs": draw_slice_pairs(jax.random.fold_in(seeds[6], 71), part),
        "perambulators": bell_draw(part_keys[5], (PAIRS, 2, NS * NV, NS * NV), 1.0, 6.0, ((0, 2), (2, 2), (3, 4))),
    }


def color_apply(link_field, vectors_here, adjoint):
    field_real = vectors_here[0].astype(jnp.float32)
    field_imag = vectors_here[1].astype(jnp.float32)
    if adjoint:
        link_real = jnp.swapaxes(link_field[0], 0, 1)
        link_imag = -jnp.swapaxes(link_field[1], 0, 1)
    else:
        link_real = link_field[0]
        link_imag = link_field[1]
    out_real = jnp.zeros(field_real.shape, jnp.float32)
    out_imag = jnp.zeros(field_real.shape, jnp.float32)
    for color_in in range(3):
        column_real = link_real[:, color_in][:, :, :, None]
        column_imag = link_imag[:, color_in][:, :, :, None]
        out_real = out_real + column_real * field_real[color_in] - column_imag * field_imag[color_in]
        out_imag = out_imag + column_real * field_imag[color_in] + column_imag * field_real[color_in]
    return jnp.stack([out_real, out_imag])

def phase_table(momenta, x_global, yz_global, extent_x, extent_y, extent_z):
    y_coord = yz_global // extent_z
    z_coord = yz_global % extent_z
    wave_x = jnp.mod(momenta[:, 0:1] * x_global[None, :], extent_x)
    wave_y = jnp.mod(momenta[:, 1:2] * y_coord[None, :], extent_y)
    wave_z = jnp.mod(momenta[:, 2:3] * z_coord[None, :], extent_z)
    numerator = wave_x[:, :, None] * (extent_y * extent_z) + (wave_y * (extent_x * extent_z) + wave_z * (extent_x * extent_y))[:, None, :]
    angle = numerator.astype(jnp.float32) * (2.0 * math.pi / (extent_x * extent_y * extent_z))
    return (jnp.cos(angle), -jnp.sin(angle))

def elemental_terms(vectors_here, forward, backward, rot_real, rot_imag, displacement):
    vector_count = vectors_here.shape[-1]
    field_real = vectors_here[0].reshape(-1, vector_count)
    field_imag = vectors_here[1].reshape(-1, vector_count)
    tops = []
    bottoms = []
    for which in range(displacement.shape[0]):
        forward_mask = (displacement[which] == 1).astype(jnp.float32)
        moved_real = forward_mask * forward[0] + (1.0 - forward_mask) * backward[0]
        moved_imag = forward_mask * forward[1] + (1.0 - forward_mask) * backward[1]
        cosine = rot_real[which][None, :, :, None]
        sine = rot_imag[which][None, :, :, None]
        phased_real = (cosine * moved_real - sine * moved_imag).astype(jnp.bfloat16).reshape(-1, vector_count)
        phased_imag = (cosine * moved_imag + sine * moved_real).astype(jnp.bfloat16).reshape(-1, vector_count)
        tops += [phased_real, phased_imag]
        bottoms += [phased_imag, -phased_real]
    top_block = jnp.concatenate(tops, axis=1)
    bottom_block = jnp.concatenate(bottoms, axis=1)
    numbers = (((0,), (0,)), ((), ()))
    first = lax.dot_general(field_real, top_block, numbers, preferred_element_type=jnp.float32)
    second = lax.dot_general(field_imag, bottom_block, numbers, preferred_element_type=jnp.float32)
    return first + second

def reference(eigenvectors, gauge_links, momenta, displacement, slice_pairs, perambulators):
    normalize = 1.0 / math.sqrt(3072 * LX * LY * LZ)
    yz_global = jnp.arange(LY * LZ, dtype=jnp.int32)

    def one_slice(slice_args):
        field_all, link_all = slice_args

        def plane_step(carry, plane_index):
            after = ((plane_index + 1) % LX).astype(jnp.int32)
            before = ((plane_index + LX - 1) % LX).astype(jnp.int32)
            here = lax.dynamic_slice_in_dim(field_all, plane_index, 1, 2)
            ahead = lax.dynamic_slice_in_dim(field_all, after, 1, 2)
            behind = lax.dynamic_slice_in_dim(field_all, before, 1, 2)
            link_here = lax.dynamic_slice_in_dim(link_all, plane_index, 1, 3)
            link_behind = lax.dynamic_slice_in_dim(link_all, before, 1, 3)
            forward = color_apply(link_here, ahead, False)
            back_local = lax.optimization_barrier(color_apply(link_behind, behind, True).astype(jnp.bfloat16))
            backward = back_local.astype(jnp.float32)
            rot_real, rot_imag = phase_table(momenta, plane_index[None], yz_global, LX, LY, LZ)
            return (carry + elemental_terms(here, forward, backward, rot_real, rot_imag, displacement), None)
        start_sum = jnp.zeros((NV, 4 * NV), jnp.float32)
        summed, _ = lax.scan(plane_step, start_sum, jnp.arange(LX, dtype=jnp.int32))
        return (summed * normalize).astype(jnp.bfloat16)
    elemental_table = lax.map(one_slice, (eigenvectors, gauge_links))

    def one_pair(pair_args):
        pair_row, block = pair_args
        sink = lax.dynamic_index_in_dim(elemental_table, pair_row[0], 0, keepdims=False).astype(jnp.float32)
        source = lax.dynamic_index_in_dim(elemental_table, pair_row[1], 0, keepdims=False).astype(jnp.float32)
        sink_real = sink[:, :NV]
        sink_imag = sink[:, NV:2 * NV]
        source_real = source[:, 2 * NV:3 * NV]
        source_imag = source[:, 3 * NV:]
        block_real = block[0].astype(jnp.float32).reshape(NS, NV, NS * NV)
        block_imag = block[1].astype(jnp.float32).reshape(NS, NV, NS * NV)
        left_real = jnp.einsum('vu,suj->svj', sink_real, block_real) - jnp.einsum('vu,suj->svj', sink_imag, block_imag)
        left_imag = jnp.einsum('vu,suj->svj', sink_real, block_imag) + jnp.einsum('vu,suj->svj', sink_imag, block_real)
        left_block = jnp.stack([left_real, left_imag]).reshape(2, NS * NV, NV, NS)
        left_block = lax.optimization_barrier(left_block.astype(jnp.bfloat16)).astype(jnp.float32)
        out_real = jnp.einsum('rvs,vw->rws', left_block[0], source_real) - jnp.einsum('rvs,vw->rws', left_block[1], source_imag)
        out_imag = jnp.einsum('rvs,vw->rws', left_block[0], source_imag) + jnp.einsum('rvs,vw->rws', left_block[1], source_real)
        return jnp.stack([out_real, out_imag]).reshape(2, NS * NV, NV * NS).astype(jnp.bfloat16)
    return lax.map(one_pair, (slice_pairs, perambulators))
```

```python
import functools
import math

import jax
import jax.numpy as jnp
from jax import lax
from jax.experimental import pallas as pl
from jax.experimental.pallas import tpu as pltpu
from jax.sharding import PartitionSpec as P

NS = 4
LY = 32
LZ = 32
MESH = pl.DeviceIdType.MESH
F32 = jnp.float32
BF16 = jnp.bfloat16
SITES = 16


def phase_table(momenta, x_global, yz_global, extent_x, extent_y, extent_z):
    y_coord = yz_global // extent_z
    z_coord = yz_global % extent_z
    wave_x = jnp.mod(momenta[:, 0:1] * x_global, extent_x)
    wave_y = jnp.mod(momenta[:, 1:2] * y_coord[None, :], extent_y)
    wave_z = jnp.mod(momenta[:, 2:3] * z_coord[None, :], extent_z)
    numerator = (
        wave_x[:, :, None] * (extent_y * extent_z)
        + (wave_y * (extent_x * extent_z) + wave_z * (extent_x * extent_y))[:, None, :]
    )
    angle = numerator.astype(F32) * (2.0 * math.pi / (extent_x * extent_y * extent_z))
    return (jnp.cos(angle), -jnp.sin(angle))


def remote(src, dst, send, recv, device):
    return pltpu.make_async_remote_copy(
        src_ref=src,
        dst_ref=dst,
        send_sem=send,
        recv_sem=recv,
        device_id=device,
        device_id_type=MESH,
    )


def dot(a, b, dims=((1,), (0,))):
    return lax.dot_general(a, b, (dims, ((), ())), preferred_element_type=F32)


def kernel(
    n, tiles, cores, normalize,
    v_ref, w_ref, p_ref, pairs_ref, disp_ref, out_ref,
    halo, ccat, wt, acc, parts, core_send, core_recv, total, rs_recv, table, pg, kbuf, rbuf,
    halo_sem, p_send, p_recv, core_sem, rs_send, rs_recv_sem, ag_send, ag_recv, bc_send, bc_recv,
):
    slab = lax.axis_index("slab")
    tile = lax.axis_index("tile")
    core = lax.axis_index("spin")
    _, _, planes, sites, nv = v_ref.shape
    pair_count, _, rows, cols = p_ref.shape
    quarter = nv // n
    others = [(dt, dc) for dt in range(tiles) for dc in range(cores) if (dt, dc) != (0, 0)]

    def along(d):
        return {"slab": lax.rem(slab + d, n)}

    def across(dt, dc):
        return {"tile": lax.rem(tile + dt, tiles), "spin": lax.rem(core + dc, cores)}

    barrier = pltpu.get_barrier_semaphore()
    for d in range(1, n):
        pl.semaphore_signal(barrier, inc=1, device_id=along(d), device_id_type=MESH)
    for dt, dc in others:
        pl.semaphore_signal(barrier, inc=1, device_id=across(dt, dc), device_id_type=MESH)
    pl.semaphore_wait(barrier, n - 1 + len(others))

    halo_copy = remote(
        v_ref.at[:, :, 0], halo, halo_sem.at[0], halo_sem.at[1], along(n - 1)
    )
    halo_copy.start()

    for plane in range(planes):
        wt[plane] = w_ref[plane].T

    for plane in range(planes):

        @pl.loop(0, sites // SITES)
        def _(i):
            here = pl.ds(pl.multiple_of(i * SITES, SITES), SITES)
            field = [
                [v_ref[part, c, plane, here, :].astype(F32) for part in range(2)]
                for c in range(3)
            ]
            weights = wt[plane, here, :]
            for e in range(2):
                for c_out in range(3):
                    real = None
                    imag = None
                    for c in range(3):
                        at = ((e * 3 + c_out) * 3 + c) * 2
                        w_real = weights[:, at : at + 1]
                        w_imag = weights[:, at + 1 : at + 2]
                        r = w_real * field[c][0] - w_imag * field[c][1]
                        m = w_real * field[c][1] + w_imag * field[c][0]
                        real = r if real is None else real + r
                        imag = m if imag is None else imag + m
                    ccat[plane * 3 + c_out, here, 2 * e * nv : (2 * e + 1) * nv] = real.astype(BF16)
                    ccat[plane * 3 + c_out, here, (2 * e + 1) * nv : (2 * e + 2) * nv] = imag.astype(BF16)

    acc[...] = jnp.zeros_like(acc)
    for plane in range(planes - 1):

        @pl.loop(0, 3)
        def _(c):
            for part in range(2):
                acc[part] += dot(
                    v_ref[part, c, plane + 1], ccat[plane * 3 + c], ((0,), (0,))
                )

    halo_copy.wait_send()
    p_copies = []
    for d in range(1, n):
        copy = remote(p_ref, pg.at[d - 1], p_send.at[d - 1], p_recv.at[d - 1], along(d))
        copy.start()
        p_copies.append(copy)
    halo_copy.wait_recv()

    @pl.loop(0, 3)
    def _(c):
        for part in range(2):
            acc[part] += dot(halo[part, c], ccat[(planes - 1) * 3 + c], ((0,), (0,)))

    for e in range(2):
        re_at = slice(2 * e * nv, (2 * e + 1) * nv)
        im_at = slice((2 * e + 1) * nv, (2 * e + 2) * nv)
        real = (acc[0, :, re_at] + acc[1, :, im_at]) * normalize
        imag = (acc[1, :, re_at] - acc[0, :, im_at]) * normalize
        forward = jnp.full((nv, nv), disp_ref[e], jnp.int32) == 1
        if e == 0:
            parts[0, e] = jnp.where(forward, real.T, real)
            parts[1, e] = jnp.where(forward, imag.T, -imag)
        else:
            parts[0, e] = jnp.where(forward, real, real.T)
            parts[1, e] = jnp.where(forward, imag, -imag.T)

    core_send[...] = parts[1 - core].astype(BF16)
    core_copy = remote(
        core_send, core_recv, core_sem.at[0], core_sem.at[1], {"spin": 1 - core}
    )
    core_copy.start()
    core_copy.wait_recv()
    total[...] = (parts[core] + core_recv[...].astype(F32)).astype(BF16)

    rs_copies = []
    for d in range(1, n):
        there = lax.rem(slab + d, n)
        copy = remote(
            total.at[:, pl.ds(pl.multiple_of(there * quarter, quarter), quarter)],
            rs_recv.at[d - 1],
            rs_send.at[d - 1],
            rs_recv_sem.at[d - 1],
            along(d),
        )
        copy.start()
        rs_copies.append(copy)
    mine = pl.ds(pl.multiple_of(slab * quarter, quarter), quarter)
    piece = total[:, mine, :].astype(F32)
    for d in range(1, n):
        rs_copies[d - 1].wait_recv()
        piece = piece + rs_recv[d - 1].astype(F32)
    piece = piece.astype(BF16)
    table[tile, core, mine, :] = piece[0]
    table[tile, core, nv:, :] = piece[1]

    ag_copies = []
    for d in range(1, n):
        own = table.at[tile, core, mine]
        copy = remote(own, own, ag_send.at[d - 1], ag_recv.at[d - 1], along(d))
        copy.start()
        ag_copies.append(copy)
    for copy in ag_copies:
        copy.wait_recv()
    bc_copies = []
    for i, (dt, dc) in enumerate(others):
        own = table.at[tile, core]
        copy = remote(own, own, bc_send.at[i], bc_recv.at[i], across(dt, dc))
        copy.start()
        bc_copies.append(copy)
    for copy in bc_copies:
        copy.wait_recv()

    def expander(count, width):
        row = lax.broadcasted_iota(jnp.int32, (count, width), 0)
        col = lax.broadcasted_iota(jnp.int32, (count, width), 1)
        inside = (row >= NS * col) & (row < NS * col + NS)
        return jnp.where(inside, 1.0, 0.0).astype(BF16)

    spread_rows = expander(NS * nv, nv)
    spread_cols = expander(cols, quarter)
    same = (
        lax.broadcasted_iota(jnp.int32, (NS * nv, cols), 0) & (NS - 1)
    ) == (lax.broadcasted_iota(jnp.int32, (NS * nv, cols), 1) & (NS - 1))

    def select(which, part, lo, hi):
        chosen = table[0, part, lo:hi, :].astype(F32)
        for t in range(1, tiles):
            here = jnp.full((hi - lo, nv), which, jnp.int32) == t
            chosen = jnp.where(here, table[t, part, lo:hi, :].astype(F32), chosen)
        return chosen.astype(BF16)

    @pl.loop(0, pair_count)
    def _(p):
        source = pairs_ref[p, 1]
        for part in range(2):
            narrow = select(source, part, nv, nv + quarter)
            wide = dot(spread_cols, narrow).astype(BF16)
            full = dot(spread_rows, wide, ((1,), (1,)))
            kbuf[p, part] = jnp.where(same, full, 0.0).astype(BF16)

    for d in range(n):
        k = lax.rem(slab + n - d, n)
        if d:
            p_copies[d - 1].wait_recv()
        block = pl.ds(pl.multiple_of(k * cols, cols), cols)

        @pl.loop(0, pair_count)
        def _(p):
            if d:
                p_real, p_imag = pg[d - 1, p, 0], pg[d - 1, p, 1]
            else:
                p_real, p_imag = p_ref[p, 0], p_ref[p, 1]
            k_real = kbuf[p, 0, block, :]
            k_imag = kbuf[p, 1, block, :]
            real = dot(p_real, k_real) - dot(p_imag, k_imag)
            imag = dot(p_real, k_imag) + dot(p_imag, k_real)
            if d:
                rbuf[p, 0] += real
                rbuf[p, 1] += imag
            else:
                rbuf[p, 0] = real
                rbuf[p, 1] = imag

    @pl.loop(0, pair_count)
    def _(p):
        sink = pairs_ref[p, 0]
        e_real = select(sink, 0, 0, nv)
        e_imag = select(sink, 1, 0, nv)
        for a in range(rows // nv):
            at = slice(a * nv, (a + 1) * nv)
            r_real = rbuf[p, 0, at, :].astype(BF16)
            r_imag = rbuf[p, 1, at, :].astype(BF16)
            out_ref[p, 0, at, :] = (dot(e_real, r_real) - dot(e_imag, r_imag)).astype(BF16)
            out_ref[p, 1, at, :] = (dot(e_real, r_imag) + dot(e_imag, r_real)).astype(BF16)

    for copy in p_copies + [core_copy] + rs_copies + ag_copies + bc_copies:
        copy.wait_send()


def link_weights(link_field, momenta, displacement, planes, sites, lattice_x):
    x_global = lax.axis_index("slab") * planes + jnp.arange(planes, dtype=jnp.int32)
    yz_global = lax.axis_index("spin") * sites + jnp.arange(sites, dtype=jnp.int32)
    forward = displacement == 1
    x_used = x_global[None, :] + jnp.where(forward, 0, 1)[:, None]
    cosine, minus_sine = phase_table(momenta, x_used, yz_global, lattice_x, LY, LZ)
    psi_imag = jnp.where(forward[:, None, None], -minus_sine, minus_sine)
    psi_real = cosine[:, None, None]
    psi_imag = psi_imag[:, None, None]
    u_real = jnp.swapaxes(link_field[0], 0, 1)[None]
    u_imag = -jnp.swapaxes(link_field[1], 0, 1)[None]
    w_real = psi_real * u_real - psi_imag * u_imag
    w_imag = psi_real * u_imag + psi_imag * u_real
    both = jnp.stack([w_real, w_imag], axis=3)
    flat = both.reshape(-1, planes, sites).transpose(1, 0, 2)
    return jnp.pad(flat, ((0, 0), (0, -flat.shape[1] % 8), (0, 0)))


def body(mesh, eigenvectors, gauge_links, momenta, displacement, slice_pairs, perambulators):
    n, tiles, cores = (mesh.shape[name] for name in ("slab", "tile", "spin"))
    field = eigenvectors[0]
    _, _, planes, sites, nv = field.shape
    pair_count, _, rows, cols = perambulators.shape
    lattice_x = planes * n
    normalize = 1.0 / math.sqrt(3072 * lattice_x * LY * LZ)
    weights = link_weights(gauge_links[0], momenta, displacement, planes, sites, lattice_x)
    quarter = nv // n
    dma = pltpu.SemaphoreType.DMA
    flops = 2 * (planes * 3 * sites * nv * nv * 8 + pair_count * 4 * rows * n * cols * cols)
    return pl.pallas_call(
        functools.partial(kernel, n, tiles, cores, normalize),
        out_shape=jax.ShapeDtypeStruct(perambulators.shape, BF16),
        in_specs=[pl.BlockSpec(memory_space=pltpu.VMEM)] * 3
        + [pl.BlockSpec(memory_space=pltpu.SMEM)] * 2,
        out_specs=pl.BlockSpec(memory_space=pltpu.VMEM),
        scratch_shapes=[
            pltpu.VMEM((2, 3, sites, nv), BF16),
            pltpu.VMEM((planes * 3, sites, 4 * nv), BF16),
            pltpu.VMEM((planes, sites, weights.shape[1]), F32),
            pltpu.VMEM((2, nv, 4 * nv), F32),
            pltpu.VMEM((2, 2, nv, nv), F32),
            pltpu.VMEM((2, nv, nv), BF16),
            pltpu.VMEM((2, nv, nv), BF16),
            pltpu.VMEM((2, nv, nv), BF16),
            pltpu.VMEM((n - 1, 2, quarter, nv), BF16),
            pltpu.VMEM((tiles, cores, nv + quarter, nv), BF16),
            pltpu.VMEM((n - 1,) + perambulators.shape, BF16),
            pltpu.VMEM((pair_count, 2, n * cols, cols), BF16),
            pltpu.VMEM((pair_count, 2, rows, cols), F32),
            dma((2,)),
            dma((n - 1,)),
            dma((n - 1,)),
            dma((2,)),
            dma((n - 1,)),
            dma((n - 1,)),
            dma((n - 1,)),
            dma((n - 1,)),
            dma((tiles * cores - 1,)),
            dma((tiles * cores - 1,)),
        ],
        compiler_params=pltpu.CompilerParams(
            collective_id=0, has_side_effects=True, vmem_limit_bytes=56 * 1024 * 1024
        ),
        cost_estimate=pl.CostEstimate(flops=flops, bytes_accessed=8 << 20, transcendentals=0),
    )(field, weights, perambulators, slice_pairs, displacement)


def solution(mesh):
    return jax.shard_map(
        functools.partial(body, mesh),
        mesh=mesh,
        in_specs=(
            P(("cfg", "tile"), None, None, "slab", "spin", None),
            P(("cfg", "tile"), None, None, None, "slab", "spin"),
            P(),
            P(),
            P("tile", None),
            P(("cfg", "tile"), None, "spin", "slab"),
        ),
        out_specs=P(("cfg", "tile"), None, "spin", "slab"),
        check_vma=False,
    )
```

```python
import functools
import math

import jax
import jax.numpy as jnp
from jax import lax
from jax.experimental import pallas as pl
from jax.experimental.pallas import tpu as pltpu
from jax.sharding import PartitionSpec as P

NS = 4
LY = 32
LZ = 32
MESH = pl.DeviceIdType.MESH
F32 = jnp.float32
BF16 = jnp.bfloat16
SITES = 16


def phase_table(momenta, x_global, yz_global, extent_x, extent_y, extent_z):
    y_coord = yz_global // extent_z
    z_coord = yz_global % extent_z
    wave_x = jnp.mod(momenta[:, 0:1] * x_global, extent_x)
    wave_y = jnp.mod(momenta[:, 1:2] * y_coord[None, :], extent_y)
    wave_z = jnp.mod(momenta[:, 2:3] * z_coord[None, :], extent_z)
    numerator = (
        wave_x[:, :, None] * (extent_y * extent_z)
        + (wave_y * (extent_x * extent_z) + wave_z * (extent_x * extent_y))[:, None, :]
    )
    angle = numerator.astype(F32) * (2.0 * math.pi / (extent_x * extent_y * extent_z))
    return (jnp.cos(angle), -jnp.sin(angle))


def remote(src, dst, send, recv, device):
    return pltpu.make_async_remote_copy(
        src_ref=src,
        dst_ref=dst,
        send_sem=send,
        recv_sem=recv,
        device_id=device,
        device_id_type=MESH,
    )


def dot(a, b, dims=((1,), (0,))):
    return lax.dot_general(a, b, (dims, ((), ())), preferred_element_type=F32)


def kernel(
    n, tiles, cores, normalize,
    v_ref, w_ref, p_ref, pairs_ref, disp_ref, out_ref,
    halo, ccat, wt, acc, parts, core_send, core_recv, total, rs_recv, table, pg, kbuf,
    part_send, part_recv,
    halo_sem, p_send, p_recv, core_sem, rs_send, rs_recv_sem, ag_send, ag_recv, x_send, x_recv,
    share_sem, end_send, end_recv,
):
    slab = lax.axis_index("slab")
    tile = lax.axis_index("tile")
    core = lax.axis_index("spin")
    _, _, planes, sites, nv = v_ref.shape
    pair_count, _, rows, cols = p_ref.shape
    quarter = nv // n
    spins = rows // nv
    chunks = [(p, a) for p in range(pair_count) for a in range(spins)]
    line = n == 4
    middle = (slab == 1) | (slab == 2)
    end = jnp.where(slab == 1, 0, n - 1)
    others = [(dt, dc) for dt in range(tiles) for dc in range(cores) if (dt, dc) != (0, 0)]

    def along(d):
        return {"slab": lax.rem(slab + d, n)}

    def gathers(who):
        return (who == 1) | (who == 2)

    def only(condition):
        return pl.when(condition) if line else (lambda f: f())

    def across(dt, dc):
        return {"tile": lax.rem(tile + dt, tiles), "spin": lax.rem(core + dc, cores)}

    barrier = pltpu.get_barrier_semaphore()
    for d in range(1, n):
        pl.semaphore_signal(barrier, inc=1, device_id=along(d), device_id_type=MESH)
    for dt, dc in others:
        pl.semaphore_signal(barrier, inc=1, device_id=across(dt, dc), device_id_type=MESH)
    pl.semaphore_wait(barrier, n - 1 + len(others))

    halo_copy = remote(
        v_ref.at[:, :, 0], halo, halo_sem.at[0], halo_sem.at[1], along(n - 1)
    )
    halo_copy.start()

    for plane in range(planes):
        wt[plane] = w_ref[plane].T

    for plane in range(planes):

        @pl.loop(0, sites // SITES)
        def _(i):
            here = pl.ds(pl.multiple_of(i * SITES, SITES), SITES)
            field = [
                [v_ref[part, c, plane, here, :].astype(F32) for part in range(2)]
                for c in range(3)
            ]
            weights = wt[plane, here, :]
            for e in range(2):
                for c_out in range(3):
                    real = None
                    imag = None
                    for c in range(3):
                        at = ((e * 3 + c_out) * 3 + c) * 2
                        w_real = weights[:, at : at + 1]
                        w_imag = weights[:, at + 1 : at + 2]
                        r = w_real * field[c][0] - w_imag * field[c][1]
                        m = w_real * field[c][1] + w_imag * field[c][0]
                        real = r if real is None else real + r
                        imag = m if imag is None else imag + m
                    ccat[plane * 3 + c_out, here, 2 * e * nv : (2 * e + 1) * nv] = real.astype(BF16)
                    ccat[plane * 3 + c_out, here, (2 * e + 1) * nv : (2 * e + 2) * nv] = imag.astype(BF16)

    acc[...] = jnp.zeros_like(acc)
    for plane in range(planes - 1):

        @pl.loop(0, 3)
        def _(c):
            for part in range(2):
                acc[part] += dot(
                    v_ref[part, c, plane + 1], ccat[plane * 3 + c], ((0,), (0,))
                )

    halo_copy.wait_send()

    def p_copy(i, d):
        p, a = chunks[i]
        return remote(
            p_ref.at[p, :, a * nv : (a + 1) * nv],
            pg.at[d - 1, p, :, a * nv : (a + 1) * nv],
            p_send.at[d - 1, i],
            p_recv.at[d - 1, i],
            along(d),
        )

    for i in range(len(chunks)):
        for d in range(1, n):

            @only(gathers(lax.rem(slab + d, n)))
            def _(i=i, d=d):
                p_copy(i, d).start()

    halo_copy.wait_recv()

    @pl.loop(0, 3)
    def _(c):
        for part in range(2):
            acc[part] += dot(halo[part, c], ccat[(planes - 1) * 3 + c], ((0,), (0,)))

    for e in range(2):
        re_at = slice(2 * e * nv, (2 * e + 1) * nv)
        im_at = slice((2 * e + 1) * nv, (2 * e + 2) * nv)
        real = (acc[0, :, re_at] + acc[1, :, im_at]) * normalize
        imag = (acc[1, :, re_at] - acc[0, :, im_at]) * normalize
        forward = jnp.full((nv, nv), disp_ref[e], jnp.int32) == 1
        if e == 0:
            parts[0, e] = jnp.where(forward, real.T, real)
            parts[1, e] = jnp.where(forward, imag.T, -imag)
        else:
            parts[0, e] = jnp.where(forward, real, real.T)
            parts[1, e] = jnp.where(forward, imag, -imag.T)

    core_send[...] = parts[1 - core].astype(BF16)
    core_copy = remote(
        core_send, core_recv, core_sem.at[0], core_sem.at[1], {"spin": 1 - core}
    )
    core_copy.start()
    core_copy.wait_recv()
    total[...] = (parts[core] + core_recv[...].astype(F32)).astype(BF16)

    rs_copies = []
    for d in range(1, n):
        there = lax.rem(slab + d, n)
        copy = remote(
            total.at[:, pl.ds(pl.multiple_of(there * quarter, quarter), quarter)],
            rs_recv.at[d - 1],
            rs_send.at[d - 1],
            rs_recv_sem.at[d - 1],
            along(d),
        )
        copy.start()
        rs_copies.append(copy)
    mine = pl.ds(pl.multiple_of(slab * quarter, quarter), quarter)
    piece = total[:, mine, :].astype(F32)
    for d in range(1, n):
        rs_copies[d - 1].wait_recv()
        piece = piece + rs_recv[d - 1].astype(F32)
    piece = piece.astype(BF16)
    table[core, tile, 0, mine, :] = piece[0]
    table[core, tile, 1, mine, :] = piece[1]

    own = table.at[core, tile, :, mine]
    ag_copies = []
    for d in range(1, n):
        copy = remote(own, own, ag_send.at[d - 1], ag_recv.at[d - 1], along(d))
        copy.start()
        ag_copies.append(copy)
    x_copies = []
    for d in range(n):
        if d:
            ag_copies[d - 1].wait_recv()
        k = lax.rem(slab + n - d, n)
        held = table.at[core, tile, :, pl.ds(pl.multiple_of(k * quarter, quarter), quarter)]
        for dt in range(1, tiles):
            copy = remote(held, held, x_send.at[dt - 1, d], x_recv.at[dt - 1, d], across(dt, 0))
            copy.start()
            x_copies.append(copy)
    for copy in x_copies:
        copy.wait_recv()
    share = remote(
        table.at[core], table.at[core], share_sem.at[0], share_sem.at[1], {"spin": 1 - core}
    )
    share.start()
    share.wait_recv()

    def expander(count, width):
        row = lax.broadcasted_iota(jnp.int32, (count, width), 0)
        col = lax.broadcasted_iota(jnp.int32, (count, width), 1)
        inside = (row >= NS * col) & (row < NS * col + NS)
        return jnp.where(inside, 1.0, 0.0).astype(BF16)

    spread_rows = expander(NS * nv, nv)
    spread_cols = expander(cols, quarter)
    same = (
        lax.broadcasted_iota(jnp.int32, (NS * nv, cols), 0) & (NS - 1)
    ) == (lax.broadcasted_iota(jnp.int32, (NS * nv, cols), 1) & (NS - 1))

    def select(which, part, elemental, at, count):
        chosen = table[part, 0, elemental, at, :].astype(F32)
        for t in range(1, tiles):
            here = jnp.full((count, nv), which, jnp.int32) == t
            chosen = jnp.where(here, table[part, t, elemental, at, :].astype(F32), chosen)
        return chosen.astype(BF16)

    def widen(side, owner):
        at = pl.ds(pl.multiple_of(owner * quarter, quarter), quarter)

        @pl.loop(0, pair_count)
        def _(p):
            for part in range(2):
                narrow = select(pairs_ref[p, 1], part, 1, at, quarter)
                wide = dot(spread_cols, narrow).astype(BF16)
                full = dot(spread_rows, wide, ((1,), (1,)))
                kbuf[side, p, part] = jnp.where(same, full, 0.0).astype(BF16)

    def term(i, d, side):
        p, a = chunks[i]
        at = slice(a * nv, (a + 1) * nv)
        k = lax.rem(slab + n - d, n)
        block = pl.ds(pl.multiple_of(k * cols, cols), cols)
        if d:
            p_real, p_imag = pg[d - 1, p, 0, at, :], pg[d - 1, p, 1, at, :]
        else:
            p_real, p_imag = p_ref[p, 0, at, :], p_ref[p, 1, at, :]
        k_real = kbuf[side, p, 0, block, :]
        k_imag = kbuf[side, p, 1, block, :]
        real = dot(p_real, k_real) - dot(p_imag, k_imag)
        imag = dot(p_real, k_imag) + dot(p_imag, k_real)
        return real, imag

    def add(x, y):
        return x[0] + y[0], x[1] + y[1]

    def finish(i, right):
        p, a = chunks[i]
        at = slice(a * nv, (a + 1) * nv)
        e_real = select(pairs_ref[p, 0], 0, 0, slice(0, nv), nv)
        e_imag = select(pairs_ref[p, 0], 1, 0, slice(0, nv), nv)
        r_real = right[0].astype(BF16)
        r_imag = right[1].astype(BF16)
        out_ref[p, 0, at, :] = (dot(e_real, r_real) - dot(e_imag, r_imag)).astype(BF16)
        out_ref[p, 1, at, :] = (dot(e_real, r_imag) + dot(e_imag, r_real)).astype(BF16)

    def end_copy(i):
        return remote(
            part_send.at[i], part_recv.at[i], end_send.at[i], end_recv.at[i], {"slab": end}
        )

    @only(middle)
    def _():
        if line:
            widen(1, end)
        else:
            widen(0, slab)
        for i in range(len(chunks)):
            for d in range(1, n):
                p_copy(i, d).wait_recv()
            if line:
                toward = term(i, 0, 1)
                toward = add(toward, term(i, 2, 1))
                first = jnp.full((nv, cols), slab, jnp.int32) == 1
                low = term(i, 1, 1)
                high = term(i, n - 1, 1)
                toward = (
                    toward[0] + jnp.where(first, high[0], low[0]),
                    toward[1] + jnp.where(first, high[1], low[1]),
                )
                part_send[i, 0] = toward[0].astype(BF16)
                part_send[i, 1] = toward[1].astype(BF16)
                end_copy(i).start()
                if i == 0:
                    widen(0, slab)
            right = term(i, 0, 0)
            for d in range(1, n):
                right = add(right, term(i, d, 0))
            finish(i, right)
        if line:
            for i in range(len(chunks)):
                end_copy(i).wait_send()

    if line:

        @pl.when(jnp.logical_not(middle))
        def _():
            widen(0, slab)
            for i in range(len(chunks)):
                right = term(i, 0, 0)
                end_copy(i).wait_recv()
                rest = (part_recv[i, 0].astype(F32), part_recv[i, 1].astype(F32))
                finish(i, add(right, rest))

    for i in range(len(chunks)):
        for d in range(1, n):

            @only(gathers(lax.rem(slab + d, n)))
            def _(i=i, d=d):
                p_copy(i, d).wait_send()

    for copy in [core_copy, share] + rs_copies + ag_copies + x_copies:
        copy.wait_send()


def link_weights(link_field, momenta, displacement, planes, sites, lattice_x):
    x_global = lax.axis_index("slab") * planes + jnp.arange(planes, dtype=jnp.int32)
    yz_global = lax.axis_index("spin") * sites + jnp.arange(sites, dtype=jnp.int32)
    forward = displacement == 1
    x_used = x_global[None, :] + jnp.where(forward, 0, 1)[:, None]
    cosine, minus_sine = phase_table(momenta, x_used, yz_global, lattice_x, LY, LZ)
    psi_imag = jnp.where(forward[:, None, None], -minus_sine, minus_sine)
    psi_real = cosine[:, None, None]
    psi_imag = psi_imag[:, None, None]
    u_real = jnp.swapaxes(link_field[0], 0, 1)[None]
    u_imag = -jnp.swapaxes(link_field[1], 0, 1)[None]
    w_real = psi_real * u_real - psi_imag * u_imag
    w_imag = psi_real * u_imag + psi_imag * u_real
    both = jnp.stack([w_real, w_imag], axis=3)
    flat = both.reshape(-1, planes, sites).transpose(1, 0, 2)
    return jnp.pad(flat, ((0, 0), (0, -flat.shape[1] % 8), (0, 0)))


def body(mesh, eigenvectors, gauge_links, momenta, displacement, slice_pairs, perambulators):
    n, tiles, cores = (mesh.shape[name] for name in ("slab", "tile", "spin"))
    field = eigenvectors[0]
    _, _, planes, sites, nv = field.shape
    pair_count, _, rows, cols = perambulators.shape
    lattice_x = planes * n
    normalize = 1.0 / math.sqrt(3072 * lattice_x * LY * LZ)
    weights = link_weights(gauge_links[0], momenta, displacement, planes, sites, lattice_x)
    quarter = nv // n
    chunks = pair_count * (rows // nv)
    dma = pltpu.SemaphoreType.DMA
    flops = 2 * (planes * 3 * sites * nv * nv * 8 + pair_count * 4 * rows * n * cols * cols)
    return pl.pallas_call(
        functools.partial(kernel, n, tiles, cores, normalize),
        out_shape=jax.ShapeDtypeStruct(perambulators.shape, BF16),
        in_specs=[pl.BlockSpec(memory_space=pltpu.VMEM)] * 3
        + [pl.BlockSpec(memory_space=pltpu.SMEM)] * 2,
        out_specs=pl.BlockSpec(memory_space=pltpu.VMEM),
        scratch_shapes=[
            pltpu.VMEM((2, 3, sites, nv), BF16),
            pltpu.VMEM((planes * 3, sites, 4 * nv), BF16),
            pltpu.VMEM((planes, sites, weights.shape[1]), F32),
            pltpu.VMEM((2, nv, 4 * nv), F32),
            pltpu.VMEM((2, 2, nv, nv), F32),
            pltpu.VMEM((2, nv, nv), BF16),
            pltpu.VMEM((2, nv, nv), BF16),
            pltpu.VMEM((2, nv, nv), BF16),
            pltpu.VMEM((n - 1, 2, quarter, nv), BF16),
            pltpu.VMEM((cores, tiles, 2, nv, nv), BF16),
            pltpu.VMEM((n - 1,) + perambulators.shape, BF16),
            pltpu.VMEM((2, pair_count, 2, n * cols, cols), BF16),
            pltpu.VMEM((chunks, 2, nv, cols), BF16),
            pltpu.VMEM((chunks, 2, nv, cols), BF16),
            dma((2,)),
            dma((n - 1, chunks)),
            dma((n - 1, chunks)),
            dma((2,)),
            dma((n - 1,)),
            dma((n - 1,)),
            dma((n - 1,)),
            dma((n - 1,)),
            dma((tiles - 1, n)),
            dma((tiles - 1, n)),
            dma((2,)),
            dma((chunks,)),
            dma((chunks,)),
        ],
        compiler_params=pltpu.CompilerParams(
            collective_id=0, has_side_effects=True, vmem_limit_bytes=56 * 1024 * 1024
        ),
        cost_estimate=pl.CostEstimate(flops=flops, bytes_accessed=8 << 20, transcendentals=0),
    )(field, weights, perambulators, slice_pairs, displacement)


def solution(mesh):
    return jax.shard_map(
        functools.partial(body, mesh),
        mesh=mesh,
        in_specs=(
            P(("cfg", "tile"), None, None, "slab", "spin", None),
            P(("cfg", "tile"), None, None, None, "slab", "spin"),
            P(),
            P(),
            P("tile", None),
            P(("cfg", "tile"), None, "spin", "slab"),
        ),
        out_specs=P(("cfg", "tile"), None, "spin", "slab"),
        check_vma=False,
    )
```

```python
import functools
import math

import jax
import jax.numpy as jnp
from jax import lax
from jax.experimental import pallas as pl
from jax.experimental.pallas import tpu as pltpu
from jax.sharding import PartitionSpec as P

NS = 4
LY = 32
LZ = 32
MESH = pl.DeviceIdType.MESH
F32 = jnp.float32
BF16 = jnp.bfloat16
SITES = 16


def phase_table(momenta, x_global, yz_global, extent_x, extent_y, extent_z):
    y_coord = yz_global // extent_z
    z_coord = yz_global % extent_z
    wave_x = jnp.mod(momenta[:, 0:1] * x_global, extent_x)
    wave_y = jnp.mod(momenta[:, 1:2] * y_coord[None, :], extent_y)
    wave_z = jnp.mod(momenta[:, 2:3] * z_coord[None, :], extent_z)
    numerator = (
        wave_x[:, :, None] * (extent_y * extent_z)
        + (wave_y * (extent_x * extent_z) + wave_z * (extent_x * extent_y))[:, None, :]
    )
    angle = numerator.astype(F32) * (2.0 * math.pi / (extent_x * extent_y * extent_z))
    return (jnp.cos(angle), -jnp.sin(angle))


def remote(src, dst, send, recv, device):
    return pltpu.make_async_remote_copy(
        src_ref=src,
        dst_ref=dst,
        send_sem=send,
        recv_sem=recv,
        device_id=device,
        device_id_type=MESH,
    )


def dot(a, b, dims=((1,), (0,))):
    return lax.dot_general(a, b, (dims, ((), ())), preferred_element_type=F32)


def kernel(
    n, tiles, cores, normalize,
    v_ref, w_ref, p_ref, pairs_ref, disp_ref, out_ref,
    halo, ccat, wt, acc, parts, core_send, core_recv, total, rs_recv, table, pg, kbuf,
    part_send, part_recv,
    halo_sem, p_send, p_recv, core_sem, rs_send, rs_recv_sem, ag_send, ag_recv, x_send, x_recv,
    share_sem, end_send, end_recv,
):
    slab = lax.axis_index("slab")
    tile = lax.axis_index("tile")
    core = lax.axis_index("spin")
    _, _, planes, sites, nv = v_ref.shape
    pair_count, _, rows, cols = p_ref.shape
    quarter = nv // n
    spins = rows // nv
    chunks = [(p, a) for p in range(pair_count) for a in range(spins)]
    line = n == 4
    middle = (slab == 1) | (slab == 2)
    end = jnp.where(slab == 1, 0, n - 1)
    others = [(dt, dc) for dt in range(tiles) for dc in range(cores) if (dt, dc) != (0, 0)]

    def along(d):
        return {"slab": lax.rem(slab + d, n)}

    def gathers(who):
        return (who == 1) | (who == 2)

    def only(condition):
        return pl.when(condition) if line else (lambda f: f())

    def across(dt, dc):
        return {"tile": lax.rem(tile + dt, tiles), "spin": lax.rem(core + dc, cores)}

    barrier = pltpu.get_barrier_semaphore()
    for d in range(1, n):
        pl.semaphore_signal(barrier, inc=1, device_id=along(d), device_id_type=MESH)
    for dt, dc in others:
        pl.semaphore_signal(barrier, inc=1, device_id=across(dt, dc), device_id_type=MESH)
    pl.semaphore_wait(barrier, n - 1 + len(others))

    halo_copies = []
    for c in range(3):
        copy = remote(
            v_ref.at[:, c, 0], halo.at[:, c], halo_sem.at[0, c], halo_sem.at[1, c], along(n - 1)
        )
        copy.start()
        halo_copies.append(copy)

    for plane in range(planes):
        wt[plane] = w_ref[plane].T

    for plane in range(planes):

        @pl.loop(0, sites // SITES)
        def _(i):
            here = pl.ds(pl.multiple_of(i * SITES, SITES), SITES)
            field = [
                [v_ref[part, c, plane, here, :].astype(F32) for part in range(2)]
                for c in range(3)
            ]
            weights = wt[plane, here, :]
            for e in range(2):
                for c_out in range(3):
                    real = None
                    imag = None
                    for c in range(3):
                        at = ((e * 3 + c_out) * 3 + c) * 2
                        w_real = weights[:, at : at + 1]
                        w_imag = weights[:, at + 1 : at + 2]
                        r = w_real * field[c][0] - w_imag * field[c][1]
                        m = w_real * field[c][1] + w_imag * field[c][0]
                        real = r if real is None else real + r
                        imag = m if imag is None else imag + m
                    ccat[plane * 3 + c_out, here, 2 * e * nv : (2 * e + 1) * nv] = real.astype(BF16)
                    ccat[plane * 3 + c_out, here, (2 * e + 1) * nv : (2 * e + 2) * nv] = imag.astype(BF16)

    acc[...] = jnp.zeros_like(acc)
    for plane in range(planes - 1):

        @pl.loop(0, 3)
        def _(c):
            for part in range(2):
                acc[part] += dot(
                    v_ref[part, c, plane + 1], ccat[plane * 3 + c], ((0,), (0,))
                )

    for copy in halo_copies:
        copy.wait_send()

    def p_copy(i, d):
        p, a = chunks[i]
        return remote(
            p_ref.at[p, :, a * nv : (a + 1) * nv],
            pg.at[d - 1, p, :, a * nv : (a + 1) * nv],
            p_send.at[d - 1, i],
            p_recv.at[d - 1, i],
            along(d),
        )

    def p_start(which):
        for i in which:
            for d in range(1, n):

                @only(gathers(lax.rem(slab + d, n)))
                def _(i=i, d=d):
                    p_copy(i, d).start()

    p_start(range(1))

    for c in range(3):
        halo_copies[c].wait_recv()
        for part in range(2):
            acc[part] += dot(halo[part, c], ccat[(planes - 1) * 3 + c], ((0,), (0,)))

    for e in range(2):
        re_at = slice(2 * e * nv, (2 * e + 1) * nv)
        im_at = slice((2 * e + 1) * nv, (2 * e + 2) * nv)
        real = (acc[0, :, re_at] + acc[1, :, im_at]) * normalize
        imag = (acc[1, :, re_at] - acc[0, :, im_at]) * normalize
        forward = jnp.full((nv, nv), disp_ref[e], jnp.int32) == 1
        if e == 0:
            parts[0, e] = jnp.where(forward, real.T, real)
            parts[1, e] = jnp.where(forward, imag.T, -imag)
        else:
            parts[0, e] = jnp.where(forward, real, real.T)
            parts[1, e] = jnp.where(forward, imag, -imag.T)

    core_send[...] = parts[1 - core].astype(BF16)
    core_copy = remote(
        core_send, core_recv, core_sem.at[0], core_sem.at[1], {"spin": 1 - core}
    )
    core_copy.start()
    core_copy.wait_recv()
    total[...] = (parts[core] + core_recv[...].astype(F32)).astype(BF16)

    rs_copies = []
    for d in range(1, n):
        there = lax.rem(slab + d, n)
        copy = remote(
            total.at[:, pl.ds(pl.multiple_of(there * quarter, quarter), quarter)],
            rs_recv.at[d - 1],
            rs_send.at[d - 1],
            rs_recv_sem.at[d - 1],
            along(d),
        )
        copy.start()
        rs_copies.append(copy)
    mine = pl.ds(pl.multiple_of(slab * quarter, quarter), quarter)
    piece = total[:, mine, :].astype(F32)
    for d in range(1, n):
        rs_copies[d - 1].wait_recv()
        piece = piece + rs_recv[d - 1].astype(F32)
    piece = piece.astype(BF16)
    table[core, tile, 0, mine, :] = piece[0]
    table[core, tile, 1, mine, :] = piece[1]

    own = table.at[core, tile, :, mine]
    ag_copies = []
    for d in range(1, n):
        copy = remote(own, own, ag_send.at[d - 1], ag_recv.at[d - 1], along(d))
        copy.start()
        ag_copies.append(copy)
    p_start(range(1, 2))
    x_copies = []
    for d in range(n):
        if d:
            ag_copies[d - 1].wait_recv()
        k = lax.rem(slab + n - d, n)
        held = table.at[core, tile, :, pl.ds(pl.multiple_of(k * quarter, quarter), quarter)]
        for dt in range(1, tiles):
            copy = remote(held, held, x_send.at[dt - 1, d], x_recv.at[dt - 1, d], across(dt, 0))
            copy.start()
            x_copies.append(copy)
    p_start(range(2, len(chunks)))
    for copy in x_copies:
        copy.wait_recv()
    share = remote(
        table.at[core], table.at[core], share_sem.at[0], share_sem.at[1], {"spin": 1 - core}
    )
    share.start()
    share.wait_recv()

    def expander(count, width):
        row = lax.broadcasted_iota(jnp.int32, (count, width), 0)
        col = lax.broadcasted_iota(jnp.int32, (count, width), 1)
        inside = (row >= NS * col) & (row < NS * col + NS)
        return jnp.where(inside, 1.0, 0.0).astype(BF16)

    spread_rows = expander(NS * nv, nv)
    spread_cols = expander(cols, quarter)
    same = (
        lax.broadcasted_iota(jnp.int32, (NS * nv, cols), 0) & (NS - 1)
    ) == (lax.broadcasted_iota(jnp.int32, (NS * nv, cols), 1) & (NS - 1))

    def select(which, part, elemental, at, count):
        chosen = table[part, 0, elemental, at, :].astype(F32)
        for t in range(1, tiles):
            here = jnp.full((count, nv), which, jnp.int32) == t
            chosen = jnp.where(here, table[part, t, elemental, at, :].astype(F32), chosen)
        return chosen.astype(BF16)

    def widen(side, owner):
        at = pl.ds(pl.multiple_of(owner * quarter, quarter), quarter)

        @pl.loop(0, pair_count)
        def _(p):
            for part in range(2):
                narrow = select(pairs_ref[p, 1], part, 1, at, quarter)
                wide = dot(spread_cols, narrow).astype(BF16)
                full = dot(spread_rows, wide, ((1,), (1,)))
                kbuf[side, p, part] = jnp.where(same, full, 0.0).astype(BF16)

    def term(i, d, side):
        p, a = chunks[i]
        at = slice(a * nv, (a + 1) * nv)
        k = lax.rem(slab + n - d, n)
        block = pl.ds(pl.multiple_of(k * cols, cols), cols)
        if not isinstance(d, int) or d:
            p_real, p_imag = pg[d - 1, p, 0, at, :], pg[d - 1, p, 1, at, :]
        else:
            p_real, p_imag = p_ref[p, 0, at, :], p_ref[p, 1, at, :]
        k_real = kbuf[side, p, 0, block, :]
        k_imag = kbuf[side, p, 1, block, :]
        real = dot(p_real, k_real) - dot(p_imag, k_imag)
        imag = dot(p_real, k_imag) + dot(p_imag, k_real)
        return real, imag

    def add(x, y):
        return x[0] + y[0], x[1] + y[1]

    def finish(i, right):
        p, a = chunks[i]
        at = slice(a * nv, (a + 1) * nv)
        e_real = select(pairs_ref[p, 0], 0, 0, slice(0, nv), nv)
        e_imag = select(pairs_ref[p, 0], 1, 0, slice(0, nv), nv)
        r_real = right[0].astype(BF16)
        r_imag = right[1].astype(BF16)
        out_ref[p, 0, at, :] = (dot(e_real, r_real) - dot(e_imag, r_imag)).astype(BF16)
        out_ref[p, 1, at, :] = (dot(e_real, r_imag) + dot(e_imag, r_real)).astype(BF16)

    def end_copy(i):
        return remote(
            part_send.at[i], part_recv.at[i], end_send.at[i], end_recv.at[i], {"slab": end}
        )

    @only(middle)
    def _():
        if line:
            widen(1, end)
        else:
            widen(0, slab)
        for i in range(len(chunks)):
            for d in range(1, n):
                p_copy(i, d).wait_recv()
            if line:
                toward = term(i, 0, 1)
                toward = add(toward, term(i, 2, 1))
                toward = add(toward, term(i, jnp.where(slab == 1, n - 1, 1), 1))
                part_send[i, 0] = toward[0].astype(BF16)
                part_send[i, 1] = toward[1].astype(BF16)
                end_copy(i).start()
                if i == 0:
                    widen(0, slab)
            right = term(i, 0, 0)
            for d in range(1, n):
                right = add(right, term(i, d, 0))
            finish(i, right)
        if line:
            for i in range(len(chunks)):
                end_copy(i).wait_send()

    if line:

        @pl.when(jnp.logical_not(middle))
        def _():
            widen(0, slab)
            for i in range(len(chunks)):
                right = term(i, 0, 0)
                end_copy(i).wait_recv()
                rest = (part_recv[i, 0].astype(F32), part_recv[i, 1].astype(F32))
                finish(i, add(right, rest))

    for i in range(len(chunks)):
        for d in range(1, n):

            @only(gathers(lax.rem(slab + d, n)))
            def _(i=i, d=d):
                p_copy(i, d).wait_send()

    for copy in [core_copy, share] + rs_copies + ag_copies + x_copies:
        copy.wait_send()


def link_weights(link_field, momenta, displacement, planes, sites, lattice_x):
    x_global = lax.axis_index("slab") * planes + jnp.arange(planes, dtype=jnp.int32)
    yz_global = lax.axis_index("spin") * sites + jnp.arange(sites, dtype=jnp.int32)
    forward = displacement == 1
    x_used = x_global[None, :] + jnp.where(forward, 0, 1)[:, None]
    cosine, minus_sine = phase_table(momenta, x_used, yz_global, lattice_x, LY, LZ)
    psi_imag = jnp.where(forward[:, None, None], -minus_sine, minus_sine)
    psi_real = cosine[:, None, None]
    psi_imag = psi_imag[:, None, None]
    u_real = jnp.swapaxes(link_field[0], 0, 1)[None]
    u_imag = -jnp.swapaxes(link_field[1], 0, 1)[None]
    w_real = psi_real * u_real - psi_imag * u_imag
    w_imag = psi_real * u_imag + psi_imag * u_real
    both = jnp.stack([w_real, w_imag], axis=3)
    flat = both.reshape(-1, planes, sites).transpose(1, 0, 2)
    return jnp.pad(flat, ((0, 0), (0, -flat.shape[1] % 8), (0, 0)))


def body(mesh, eigenvectors, gauge_links, momenta, displacement, slice_pairs, perambulators):
    n, tiles, cores = (mesh.shape[name] for name in ("slab", "tile", "spin"))
    field = eigenvectors[0]
    _, _, planes, sites, nv = field.shape
    pair_count, _, rows, cols = perambulators.shape
    lattice_x = planes * n
    normalize = 1.0 / math.sqrt(3072 * lattice_x * LY * LZ)
    weights = link_weights(gauge_links[0], momenta, displacement, planes, sites, lattice_x)
    quarter = nv // n
    chunks = pair_count * (rows // nv)
    dma = pltpu.SemaphoreType.DMA
    flops = 2 * (planes * 3 * sites * nv * nv * 8 + pair_count * 4 * rows * n * cols * cols)
    return pl.pallas_call(
        functools.partial(kernel, n, tiles, cores, normalize),
        out_shape=jax.ShapeDtypeStruct(perambulators.shape, BF16),
        in_specs=[pl.BlockSpec(memory_space=pltpu.VMEM)] * 3
        + [pl.BlockSpec(memory_space=pltpu.SMEM)] * 2,
        out_specs=pl.BlockSpec(memory_space=pltpu.VMEM),
        scratch_shapes=[
            pltpu.VMEM((2, 3, sites, nv), BF16),
            pltpu.VMEM((planes * 3, sites, 4 * nv), BF16),
            pltpu.VMEM((planes, sites, weights.shape[1]), F32),
            pltpu.VMEM((2, nv, 4 * nv), F32),
            pltpu.VMEM((2, 2, nv, nv), F32),
            pltpu.VMEM((2, nv, nv), BF16),
            pltpu.VMEM((2, nv, nv), BF16),
            pltpu.VMEM((2, nv, nv), BF16),
            pltpu.VMEM((n - 1, 2, quarter, nv), BF16),
            pltpu.VMEM((cores, tiles, 2, nv, nv), BF16),
            pltpu.VMEM((n - 1,) + perambulators.shape, BF16),
            pltpu.VMEM((2, pair_count, 2, n * cols, cols), BF16),
            pltpu.VMEM((chunks, 2, nv, cols), BF16),
            pltpu.VMEM((chunks, 2, nv, cols), BF16),
            dma((2, 3)),
            dma((n - 1, chunks)),
            dma((n - 1, chunks)),
            dma((2,)),
            dma((n - 1,)),
            dma((n - 1,)),
            dma((n - 1,)),
            dma((n - 1,)),
            dma((tiles - 1, n)),
            dma((tiles - 1, n)),
            dma((2,)),
            dma((chunks,)),
            dma((chunks,)),
        ],
        compiler_params=pltpu.CompilerParams(
            collective_id=0, has_side_effects=True, vmem_limit_bytes=56 * 1024 * 1024
        ),
        cost_estimate=pl.CostEstimate(flops=flops, bytes_accessed=8 << 20, transcendentals=0),
    )(field, weights, perambulators, slice_pairs, displacement)


def solution(mesh):
    return jax.shard_map(
        functools.partial(body, mesh),
        mesh=mesh,
        in_specs=(
            P(("cfg", "tile"), None, None, "slab", "spin", None),
            P(("cfg", "tile"), None, None, None, "slab", "spin"),
            P(),
            P(),
            P("tile", None),
            P(("cfg", "tile"), None, "spin", "slab"),
        ),
        out_specs=P(("cfg", "tile"), None, "spin", "slab"),
        check_vma=False,
    )
```
